32 devices in a mesh: rows: 8 (over z, x), feat: 4 (over y, core).
Axes of the slice: x: 2, y: 2, z: 4, core: 2. Of those that a mesh axis runs over, the one named last changes fastest.
Arguments:
- bins: int32 [256, 12288], P('feat', 'rows'), may hold values from 0 to 255
- gradients: bfloat16 [12288], P('rows'), may hold values from -11 to 14
- hessians: bfloat16 [12288], P('rows'), may hold values from 0.099609375 to 1
- predictions: float32 [12288], P('rows'), may hold values from -6 to 6
- leaf: int32 [12288], P('rows'), may hold values from 0 to 7
- split_feature: int32 [8], replicated, may hold values from 0 to 255
- split_bin: int32 [8], replicated, may hold values from 0 to 254
- row_counts: int32 [8], P('rows'), may hold values from 96 to 1536, as said below
Outputs:
- hist: float32 [4, 64, 2, 16, 256], P('feat', 'rows')
- new_leaf: int32 [12288], P('rows')
- new_pred: float32 [12288], P('rows')
The draws below stay inside these ranges and needn't reach their ends.
Inputs may be any that keep to these rules, and one draw needn't show every extreme that they name: `row_counts`: some sweep batch has all 1536 rows live.
All inputs are finite; a program needn't handle non-finite values.
Results may differ from the reference program's by a relative error of at most 0.0003.
Values may be sent and summed in bfloat16 or wider, within the bound.
A program may use at most 128 MiB of HBM per device.

```python
import math
import jax
import jax.numpy as jnp
from jax import lax

F = 256
B = 256
LEAVES = 8
ROW_CAP = 1536
ROWS = 12288
N_FEAT = 4


def draw_gradients(key, part):
    count = ROWS // ROW_CAP
    shard = (jnp.arange(ROWS) // ROW_CAP).astype(jnp.float32)
    scale = 1.0 + 2.0 * shard / max(count - 1, 1)
    base = 0.6 + jax.random.truncated_normal(key, -4.0, 4.0, (ROWS,), jnp.float32)
    return (scale * base).astype(jnp.bfloat16)


def draw_row_counts(key, part):
    count = ROWS // ROW_CAP
    first = jax.random.fold_in(key, 11)
    second = jax.random.fold_in(key, 12)
    third = jax.random.fold_in(key, 13)
    base = jax.random.randint(first, (count,), ROW_CAP // 16, ROW_CAP // 2 + 1)
    full = jax.random.randint(second, (count,), 0, 8) == 0
    picked = jax.random.randint(third, (), 0, count)
    full = full | (jnp.arange(count) == picked)
    return jnp.where(full, ROW_CAP, base).astype(jnp.int32)


def touch_ends(result, own_key, smallest, top_value):
    longest = result.shape.index(max(result.shape))
    spots = []
    for shift in (0, 1):
        where = [jax.random.randint(jax.random.fold_in(own_key, axis), (), 0, length) for axis, length in enumerate(result.shape)]
        where[longest] = (where[longest] + shift) % result.shape[longest]
        spots.append(tuple(where))
    return result.at[spots[0]].set(smallest).at[spots[1]].set(top_value)


def steps_of(rng, extent, shards, low, top_value):
    gain = 1.0
    for axis_at, blocks in shards:
        draws = jax.random.uniform(jax.random.fold_in(jax.random.fold_in(rng, 6), axis_at), (blocks,), jnp.float32, low / len(shards), top_value / len(shards))
        gain = gain * jnp.repeat(jnp.exp(draws), extent[axis_at] // blocks).reshape((-1,) + (1,) * (len(extent) - 1 - axis_at))
    return gain


def gaussian(own_key, dims, width, bound, pieces=(), held_as=jnp.bfloat16):
    factor_of = steps_of(own_key, dims, pieces, -0.22, 0.18) if pieces else 1.0
    drawn = jax.random.normal(own_key, dims, jnp.float32) * width * factor_of
    return jnp.minimum(jnp.maximum(drawn, -bound), bound).astype(held_as)


def setup_inputs(seed: int = 0) -> dict:
    key_of = jax.random.split(jax.random.key(seed), 9)
    return {
        "bins": touch_ends(jax.random.randint(key_of[0], (F, ROWS), 0, B), jax.random.fold_in(key_of[0], 1), 0, B - 1).astype(jnp.int32),
        "gradients": draw_gradients(jax.random.fold_in(key_of[8], 71), 0),
        "hessians": jnp.clip(jnp.exp(math.log(1.0) - 2.306499 * jax.random.uniform(key_of[2], (ROWS,), jnp.float32) ** steps_of(key_of[2], (ROWS,), ((0, 8),), -0.2, 0.2)), 0.099609375, 1.0).astype(jnp.bfloat16),
        "predictions": gaussian(key_of[3], (ROWS,), 1.0, 6.0, ((0, 8),), jnp.float32),
        "leaf": touch_ends(jax.random.randint(key_of[4], (ROWS,), 0, LEAVES), jax.random.fold_in(key_of[4], 1), 0, LEAVES - 1).astype(jnp.int32),
        "split_feature": touch_ends(jax.random.randint(key_of[5], (LEAVES,), 0, F), jax.random.fold_in(key_of[5], 1), 0, F - 1).astype(jnp.int32),
        "split_bin": touch_ends(jax.random.randint(key_of[6], (LEAVES,), 0, B - 1), jax.random.fold_in(key_of[6], 1), 0, (B - 1) - 1).astype(jnp.int32),
        "row_counts": draw_row_counts(jax.random.fold_in(key_of[8], 71), 0),
    }


def reference(bins, gradients, hessians, predictions, leaf, split_feature, split_bin, row_counts):
    total = bins.shape[1]
    kids = 2 * LEAVES
    position = jnp.arange(total, dtype=jnp.int32)
    batch = (position // ROW_CAP).astype(jnp.int32)
    live = (position % ROW_CAP) < row_counts[batch]
    wanted = split_feature[leaf]
    cutoff = split_bin[leaf]
    chosen = jnp.take_along_axis(bins, wanted[None, :], 0)[0]
    going = jnp.where(chosen > cutoff, 1, 0).astype(jnp.int32)
    new_leaf = (2 * leaf + going).astype(jnp.int32)
    grad_live = jnp.where(live, gradients.astype(jnp.float32), jnp.float32(0.0))
    hess_live = jnp.where(live, hessians.astype(jnp.float32), jnp.float32(0.0))
    weights = jnp.stack([grad_live, hess_live], 1)

    def one_feature(column):
        index = (new_leaf * B + column).astype(jnp.int32)
        summed = jax.ops.segment_sum(weights, index, num_segments=kids * B)
        return summed.reshape(kids, B, 2).transpose(2, 0, 1)

    hist = lax.map(one_feature, bins)
    hist = hist.reshape(N_FEAT, F // N_FEAT, 2, kids, B)
    totals = jax.ops.segment_sum(weights, new_leaf, num_segments=kids)
    value = -totals[:, 0] / (totals[:, 1] + 1.0)
    new_pred = predictions + 0.5 * value[new_leaf]
    return hist, new_leaf, new_pred
```

```python
import functools

import jax
import jax.numpy as jnp
from jax import lax
from jax.experimental import pallas as pl
from jax.experimental.pallas import tpu as pltpu
from jax.sharding import PartitionSpec as P

B = 256
LANES = 128
HALF = 128
STEP = 2
MESH = pl.DeviceIdType.MESH


def round_up(value, unit):
    return -(-value // unit) * unit


def pad_rows(x, rows):
    if x.shape[0] == rows:
        return x
    return jnp.concatenate([x, jnp.zeros((rows - x.shape[0], x.shape[1]), x.dtype)], 0)


def exchange_kernel(dims, bins_ref, grad_ref, hess_ref, leaf_ref, feature_ref, bin_ref, count_ref,
                    early_ref, late_ref, out_early, out_late, flag_in,
                    flag_send, flag_recv, early_send, early_recv, late_send, late_recv):
    n_rows, n_feat, owned, padded, chunks, leaves = dims
    width = owned * n_rows
    me_r = lax.axis_index("rows")
    me_f = lax.axis_index("feat")
    small = late_ref.shape[1]
    cells = chunks * padded

    def row_peer(step):
        return lax.rem(me_r + step, n_rows)

    def feat_peer(step):
        return lax.rem(me_f + step, n_feat)

    barrier = pltpu.get_barrier_semaphore()
    for step in range(1, n_feat):
        pl.semaphore_signal(barrier, inc=1, device_id=(me_r, feat_peer(step)), device_id_type=MESH)
    for step in range(1, n_rows):
        pl.semaphore_signal(barrier, inc=1, device_id=(row_peer(step), me_f), device_id_type=MESH)

    leaf = leaf_ref[...]
    wanted = jnp.zeros(leaf.shape, jnp.int32)
    cutoff = jnp.zeros(leaf.shape, jnp.int32)
    for slot in range(leaves):
        here = leaf == slot
        wanted = jnp.where(here, feature_ref[slot], wanted)
        cutoff = jnp.where(here, bin_ref[slot], cutoff)
    local = wanted - me_f * width
    ids = lax.broadcasted_iota(jnp.int32, (width, LANES), 0)
    chosen = []
    for chunk in range(chunks):
        block = bins_ref[:, chunk * LANES:(chunk + 1) * LANES]
        hit = ids == local[chunk:chunk + 1, :]
        chosen.append(jnp.sum(jnp.where(hit, block.astype(jnp.float32), 0.0), 0, keepdims=True))
    chosen = jnp.concatenate(chosen, 0)
    mine = (local >= 0) & (local < width)
    flags = jnp.where(mine & (chosen > cutoff.astype(jnp.float32)), 1.0, 0.0)
    flag_in[me_f] = pad_rows(flags, small).astype(jnp.bfloat16)

    pl.semaphore_wait(barrier, n_feat - 1 + n_rows - 1)
    flag_copies = []
    for step in range(1, n_feat):
        copy = pltpu.make_async_remote_copy(
            src_ref=flag_in.at[me_f], dst_ref=flag_in.at[me_f],
            send_sem=flag_send.at[step - 1], recv_sem=flag_recv.at[step - 1],
            device_id=(me_r, feat_peer(step)), device_id_type=MESH)
        copy.start()
        flag_copies.append(copy)

    count = count_ref[0]
    spot = (lax.broadcasted_iota(jnp.int32, leaf.shape, 0) * LANES
            + lax.broadcasted_iota(jnp.int32, leaf.shape, 1))
    live = spot < count
    upper = jnp.full((1, LANES), count // 8, jnp.int32).astype(jnp.float32)
    lower = jnp.full((1, LANES), count % 8, jnp.int32).astype(jnp.float32)
    grad = jnp.where(live, grad_ref[...].astype(jnp.float32), 0.0)
    hess = jnp.where(live, hess_ref[...].astype(jnp.float32), 0.0)
    tail = jnp.concatenate([pad_rows(jnp.concatenate([grad, upper, lower], 0), small),
                            pad_rows(hess, small)], 0).astype(jnp.bfloat16)
    for target in range(n_rows):
        blocks = []
        for chunk in range(chunks):
            block = bins_ref[target * owned:(target + 1) * owned, chunk * LANES:(chunk + 1) * LANES]
            blocks.append(pad_rows(block.astype(jnp.float32), padded))
        packed = jnp.concatenate(blocks, 0)
        out_early[target, :cells, :] = pad_rows(packed, cells).astype(jnp.bfloat16)
        out_early[target, cells:, :] = tail
    early_copies = []
    for step in range(1, n_rows):
        copy = pltpu.make_async_remote_copy(
            src_ref=out_early.at[row_peer(step)], dst_ref=early_ref.at[me_r],
            send_sem=early_send.at[step - 1], recv_sem=early_recv.at[step - 1],
            device_id=(row_peer(step), me_f), device_id_type=MESH)
        copy.start()
        early_copies.append(copy)

    for copy in flag_copies:
        copy.wait()
    merged = jnp.zeros((small, LANES), jnp.float32)
    for slot in range(n_feat):
        merged = merged + flag_in[slot].astype(jnp.float32)
    going = jnp.where(merged > 0.5, 1.0, 0.0)
    child = 2.0 * pad_rows(leaf.astype(jnp.float32), small) + going
    out_late[...] = child.astype(jnp.bfloat16)
    late_copies = []
    for step in range(1, n_rows):
        copy = pltpu.make_async_remote_copy(
            src_ref=out_late, dst_ref=late_ref.at[me_r],
            send_sem=late_send.at[step - 1], recv_sem=late_recv.at[step - 1],
            device_id=(row_peer(step), me_f), device_id_type=MESH)
        copy.start()
        late_copies.append(copy)
    late_ref[me_r] = child.astype(jnp.bfloat16)
    early_ref[me_r] = out_early[me_r]
    for copy in early_copies + late_copies:
        copy.wait()


def histogram_kernel(dims, early_ref, late_ref, pred_ref, hist_ref, leaf_ref, new_ref, sums, tot):
    n_rows, owned, padded, chunks, kids = dims
    cells = chunks * padded
    small = late_ref.shape[1]
    sums[...] = jnp.zeros_like(sums)
    tot[...] = jnp.zeros_like(tot)
    levels = lax.broadcasted_iota(jnp.int32, (HALF, LANES), 0).astype(jnp.float32).astype(jnp.bfloat16)
    slots = lax.broadcasted_iota(jnp.int32, (kids, LANES), 0).astype(jnp.float32).astype(jnp.bfloat16)
    one = jnp.ones((), jnp.bfloat16)
    zero = jnp.zeros((), jnp.bfloat16)
    steps = []
    for batch in range(n_rows):
        held = early_ref[batch, cells:cells + small, :].astype(jnp.float32)
        count = held[chunks:chunks + 1, :] * 8.0 + held[chunks + 1:chunks + 2, :]
        count = jnp.max(count).astype(jnp.int32)
        steps.append((count + STEP * LANES - 1) // (STEP * LANES))

    for batch in range(n_rows):
        grads = early_ref[batch, cells:cells + small, :].astype(jnp.float32)
        def one_step(step, carry, batch=batch):
            start = pl.multiple_of(step * STEP * padded, STEP * padded)
            block = early_ref[batch, pl.ds(start, STEP * padded), :].astype(jnp.float32)
            high = jnp.where(block >= float(HALF), 1.0, 0.0)
            low = block - high * float(HALF)
            weights = []
            for part in range(STEP):
                chunk = step * STEP + part
                pick = lax.broadcasted_iota(jnp.int32, (small, LANES), 0) == chunk
                def row(ref_value):
                    return jnp.sum(jnp.where(pick, ref_value.astype(jnp.float32), 0.0), 0, keepdims=True).astype(jnp.bfloat16)
                child = row(late_ref[batch])
                grad = row(early_ref[batch, cells:cells + small, :])
                hess = row(early_ref[batch, cells + small:cells + 2 * small, :])
                member = slots == child
                weights.append(jnp.concatenate([jnp.where(member, grad, zero), jnp.where(member, hess, zero)], 0))
            tot[...] += sum(w.astype(jnp.float32) for w in weights)
            both = jnp.concatenate(weights, 1)
            for f in range(owned):
                hot = []
                top = []
                for part in range(STEP):
                    at = part * padded + f
                    hot.append(jnp.where(levels == low[at:at + 1, :].astype(jnp.bfloat16), one, zero))
                    top.append(jnp.broadcast_to(high[at:at + 1, :], weights[0].shape).astype(jnp.bfloat16))
                hot = jnp.concatenate(hot, 1)
                upper = both * jnp.concatenate(top, 1)
                masked = jnp.concatenate([both - upper, upper], 0)
                sums[f] += lax.dot_general(masked, hot, (((1,), (1,)), ((), ())),
                                           preferred_element_type=jnp.float32)
            return carry
        lax.fori_loop(0, steps[batch], one_step, 0)

    for f in range(owned):
        hist_ref[f, :, :HALF] = sums[f, :2 * kids, :]
        hist_ref[f, :, HALF:] = sums[f, 2 * kids:, :]
    totals = jnp.sum(tot[...], 1, keepdims=True)
    value = -totals[:kids] / (totals[kids:] + 1.0)
    me_r = lax.axis_index("rows")
    child = late_ref[me_r].astype(jnp.float32)[:chunks]
    gained = jnp.zeros(child.shape, jnp.float32)
    for kid in range(kids):
        gained = jnp.where(child == float(kid), value[kid:kid + 1, :], gained)
    leaf_ref[...] = child.astype(jnp.int32)
    new_ref[...] = pred_ref[...] + 0.5 * gained


def solution(mesh):
    n_rows, n_feat = mesh.shape["rows"], mesh.shape["feat"]
    in_specs = (P("feat", "rows"), P("rows"), P("rows"), P("rows"), P("rows"), P(), P(), P("rows"))
    out_specs = (P("feat", "rows", None, None, None), P("rows"), P("rows"))
    vmem = pl.BlockSpec(memory_space=pltpu.VMEM)
    smem = pl.BlockSpec(memory_space=pltpu.SMEM)

    def body(bins, gradients, hessians, predictions, leaf, split_feature, split_bin, row_counts):
        width, rows_here = bins.shape
        leaves = split_feature.shape[0]
        kids = 2 * leaves
        owned = width // n_rows
        padded = round_up(owned, 8)
        chunks = rows_here // LANES
        small = round_up(chunks + 2, 16)
        cells = chunks * padded
        length = cells + 2 * small
        tall = (chunks, LANES)
        bf16 = jnp.bfloat16
        early, late = pl.pallas_call(
            functools.partial(exchange_kernel, (n_rows, n_feat, owned, padded, chunks, leaves)),
            out_shape=(jax.ShapeDtypeStruct((n_rows, length, LANES), bf16),
                       jax.ShapeDtypeStruct((n_rows, small, LANES), bf16)),
            in_specs=[vmem, vmem, vmem, vmem, smem, smem, smem],
            out_specs=(vmem, vmem),
            scratch_shapes=[
                pltpu.VMEM((n_rows, length, LANES), bf16),
                pltpu.VMEM((small, LANES), bf16),
                pltpu.VMEM((n_feat, small, LANES), bf16),
                pltpu.SemaphoreType.DMA((n_feat - 1,)),
                pltpu.SemaphoreType.DMA((n_feat - 1,)),
                pltpu.SemaphoreType.DMA((n_rows - 1,)),
                pltpu.SemaphoreType.DMA((n_rows - 1,)),
                pltpu.SemaphoreType.DMA((n_rows - 1,)),
                pltpu.SemaphoreType.DMA((n_rows - 1,)),
            ],
            compiler_params=pltpu.CompilerParams(collective_id=0, has_side_effects=True),
            name="exchange_rows",
        )(bins, gradients.reshape(tall), hessians.reshape(tall), leaf.reshape(tall),
          split_feature, split_bin, row_counts)
        hist, new_leaf, new_pred = pl.pallas_call(
            functools.partial(histogram_kernel, (n_rows, owned, padded, chunks, kids)),
            out_shape=(jax.ShapeDtypeStruct((owned, 2 * kids, B), jnp.float32),
                       jax.ShapeDtypeStruct(tall, jnp.int32),
                       jax.ShapeDtypeStruct(tall, jnp.float32)),
            in_specs=[vmem, vmem, vmem],
            out_specs=(vmem, vmem, vmem),
            scratch_shapes=[pltpu.VMEM((owned, 4 * kids, HALF), jnp.float32),
                            pltpu.VMEM((2 * kids, LANES), jnp.float32)],
            name="child_histograms",
        )(early, late, predictions.reshape(tall))
        return (hist.reshape(1, owned, 2, kids, B), new_leaf.reshape(rows_here), new_pred.reshape(rows_here))

    return jax.shard_map(body, mesh=mesh, in_specs=in_specs, out_specs=out_specs, check_vma=False)
```

```python
import functools

import jax
import jax.numpy as jnp
from jax import lax
from jax.experimental import pallas as pl
from jax.experimental.pallas import tpu as pltpu
from jax.sharding import PartitionSpec as P

B = 256
LANES = 128
HALF = 128
TILE = 16
PAIR = 2
GROUP = 4
VMEM_BYTES = 16 * 1024 * 1024
MESH = pl.DeviceIdType.MESH


def round_up(value, unit):
    return -(-value // unit) * unit


def pad_rows(x, rows):
    if x.shape[0] == rows:
        return x
    return jnp.concatenate([x, jnp.zeros((rows - x.shape[0], x.shape[1]), x.dtype)], 0)


def exchange_kernel(dims, bins_hbm, grad_ref, hess_ref, leaf_ref, feature_ref, bin_ref, count_ref,
                    early_ref, late_ref, bins_ref, out_early, out_late, flag_in,
                    bins_sem, flag_send, flag_recv, early_send, early_recv, late_send, late_recv):
    n_rows, n_feat, owned, padded, chunks, leaves = dims
    width = owned * n_rows
    me_r = lax.axis_index("rows")
    me_f = lax.axis_index("feat")
    small = late_ref.shape[1]
    cells = chunks * padded

    def row_peer(step):
        return lax.rem(me_r + step, n_rows)

    def feat_peer(step):
        return lax.rem(me_f + step, n_feat)

    fetch = pltpu.make_async_copy(bins_hbm, bins_ref, bins_sem)
    fetch.start()
    barrier = pltpu.get_barrier_semaphore()
    for step in range(1, n_feat):
        pl.semaphore_signal(barrier, inc=1, device_id=(me_r, feat_peer(step)), device_id_type=MESH)
    for step in range(1, n_rows):
        pl.semaphore_signal(barrier, inc=1, device_id=(row_peer(step), me_f), device_id_type=MESH)

    leaf = leaf_ref[...]
    wanted = jnp.zeros(leaf.shape, jnp.int32)
    cutoff = jnp.zeros(leaf.shape, jnp.int32)
    for slot in range(leaves):
        here = leaf == slot
        wanted = jnp.where(here, feature_ref[slot], wanted)
        cutoff = jnp.where(here, bin_ref[slot], cutoff)
    local = wanted - me_f * width
    fetch.wait()
    ids = lax.broadcasted_iota(jnp.int32, (width, LANES), 0)
    chosen = []
    for chunk in range(chunks):
        block = bins_ref[:, chunk * LANES:(chunk + 1) * LANES]
        hit = ids == local[chunk:chunk + 1, :]
        chosen.append(jnp.sum(jnp.where(hit, block.astype(jnp.float32), 0.0), 0, keepdims=True))
    chosen = jnp.concatenate(chosen, 0)
    mine = (local >= 0) & (local < width)
    flags = jnp.where(mine & (chosen > cutoff.astype(jnp.float32)), 1.0, 0.0)
    flag_in[me_f] = pad_rows(flags, small).astype(jnp.bfloat16)

    count = count_ref[0]
    spot = (lax.broadcasted_iota(jnp.int32, leaf.shape, 0) * LANES
            + lax.broadcasted_iota(jnp.int32, leaf.shape, 1))
    live = spot < count
    upper = jnp.full((1, LANES), count // 8, jnp.int32).astype(jnp.float32)
    lower = jnp.full((1, LANES), count % 8, jnp.int32).astype(jnp.float32)
    grad = jnp.where(live, grad_ref[...].astype(jnp.float32), 0.0)
    hess = jnp.where(live, hess_ref[...].astype(jnp.float32), 0.0)
    tail = jnp.concatenate([pad_rows(jnp.concatenate([grad, upper, lower], 0), small),
                            pad_rows(hess, small)], 0).astype(jnp.bfloat16)
    for target in range(n_rows):
        blocks = []
        for chunk in range(chunks):
            block = bins_ref[target * owned:(target + 1) * owned, chunk * LANES:(chunk + 1) * LANES]
            blocks.append(pad_rows(block.astype(jnp.float32), padded))
        packed = jnp.concatenate(blocks, 0)
        out_early[target, :cells, :] = pad_rows(packed, cells).astype(jnp.bfloat16)
        out_early[target, cells:, :] = tail
    pl.semaphore_wait(barrier, n_feat - 1 + n_rows - 1)
    flag_copies = []
    for step in range(1, n_feat):
        copy = pltpu.make_async_remote_copy(
            src_ref=flag_in.at[me_f], dst_ref=flag_in.at[me_f],
            send_sem=flag_send.at[step - 1], recv_sem=flag_recv.at[step - 1],
            device_id=(me_r, feat_peer(step)), device_id_type=MESH)
        copy.start()
        flag_copies.append(copy)
    early_copies = []
    for step in range(1, n_rows):
        copy = pltpu.make_async_remote_copy(
            src_ref=out_early.at[row_peer(step)], dst_ref=early_ref.at[me_r],
            send_sem=early_send.at[step - 1], recv_sem=early_recv.at[step - 1],
            device_id=(row_peer(step), me_f), device_id_type=MESH)
        copy.start()
        early_copies.append(copy)

    for copy in flag_copies:
        copy.wait()
    merged = jnp.zeros((small, LANES), jnp.float32)
    for slot in range(n_feat):
        merged = merged + flag_in[slot].astype(jnp.float32)
    going = jnp.where(merged > 0.5, 1.0, 0.0)
    child = 2.0 * pad_rows(leaf.astype(jnp.float32), small) + going
    out_late[...] = child.astype(jnp.bfloat16)
    late_copies = []
    for step in range(1, n_rows):
        copy = pltpu.make_async_remote_copy(
            src_ref=out_late, dst_ref=late_ref.at[me_r],
            send_sem=late_send.at[step - 1], recv_sem=late_recv.at[step - 1],
            device_id=(row_peer(step), me_f), device_id_type=MESH)
        copy.start()
        late_copies.append(copy)
    late_ref[me_r] = child.astype(jnp.bfloat16)
    early_ref[me_r] = out_early[me_r]
    for copy in early_copies + late_copies:
        copy.wait()


def histogram_kernel(dims, early_ref, late_ref, pred_ref, hist_ref, leaf_ref, new_ref, held, tot, order):
    n_rows, owned, padded, chunks, kids = dims
    cells = chunks * padded
    small = late_ref.shape[1]
    bf16 = jnp.bfloat16
    units = chunks // PAIR
    hist_ref[...] = jnp.zeros_like(hist_ref)
    tot[...] = jnp.zeros_like(tot)
    held[n_rows] = jnp.zeros(held.shape[1:], jnp.float32)
    for batch in range(n_rows):
        held[batch, :2 * small, :] = early_ref[batch, cells:, :].astype(jnp.float32)
        held[batch, 2 * small:, :] = late_ref[batch].astype(jnp.float32)
    filled = jnp.int32(0)
    for batch in range(n_rows):
        count = held[batch, chunks:chunks + 1, :] * 8.0 + held[batch, chunks + 1:chunks + 2, :]
        count = jnp.max(count).astype(jnp.int32)
        for unit in range(units):
            order[filled] = batch * units + unit
            filled = filled + jnp.where(count > unit * PAIR * LANES, 1, 0).astype(jnp.int32)
    for extra in range(GROUP):
        order[filled + extra] = n_rows * units

    rows16 = lax.broadcasted_iota(jnp.int32, (TILE, LANES), 0).astype(jnp.float32)
    levels = [(rows16 + float(TILE * at)).astype(bf16) for at in range(HALF // TILE)]
    slots = lax.broadcasted_iota(jnp.int32, (kids, LANES), 0).astype(jnp.float32).astype(bf16)
    one = jnp.ones((), bf16)
    zero = jnp.zeros((), bf16)

    def one_step(step, carry):
        highs, lows, weights = [], [], []
        for part in range(GROUP):
            number = order[step * GROUP + part]
            batch = number // units
            unit = number - batch * units
            source = jnp.minimum(batch, n_rows - 1)
            start = pl.multiple_of(unit * PAIR * padded, PAIR * padded)
            block = early_ref[source, pl.ds(start, PAIR * padded), :].astype(jnp.float32)
            high = jnp.where(block >= float(HALF), 1.0, 0.0)
            low = block - high * float(HALF)
            for half in range(PAIR):
                highs.append(high[half * padded:(half + 1) * padded])
                lows.append(low[half * padded:(half + 1) * padded])
                chunk = unit * PAIR + half
                grad, hess, child = [
                    jnp.broadcast_to(held[batch, pl.ds(chunk + small * kind, 1), :], (kids, LANES)).astype(bf16)
                    for kind in range(3)]
                member = slots == child
                weights.append(jnp.concatenate([jnp.where(member, grad, zero), jnp.where(member, hess, zero)], 0))
        tot[...] += sum(w.astype(jnp.float32) for w in weights)
        both = jnp.concatenate(weights, 1)
        for f in range(owned):
            hot = []
            top = []
            for high, low in zip(highs, lows):
                level = jnp.broadcast_to(low[f:f + 1, :], (TILE, LANES)).astype(bf16)
                hot.append(jnp.concatenate([jnp.where(level == at, one, zero) for at in levels], 0))
                top.append(jnp.broadcast_to(high[f:f + 1, :], (2 * kids, LANES)).astype(bf16))
            hot = jnp.concatenate(hot, 1)
            upper = both * jnp.concatenate(top, 1)
            masked = jnp.concatenate([both - upper, upper], 0)
            found = lax.dot_general(masked, hot, (((1,), (1,)), ((), ())),
                                    preferred_element_type=jnp.float32)
            hist_ref[f, :, :HALF] += found[:2 * kids]
            hist_ref[f, :, HALF:] += found[2 * kids:]
        return carry

    lax.fori_loop(0, (filled + GROUP - 1) // GROUP, one_step, 0)

    totals = jnp.sum(tot[...], 1, keepdims=True)
    value = -totals[:kids] / (totals[kids:] + 1.0)
    me_r = lax.axis_index("rows")
    child = held[me_r, 2 * small:2 * small + chunks, :]
    gained = jnp.zeros(child.shape, jnp.float32)
    for kid in range(kids):
        gained = jnp.where(child == float(kid), value[kid:kid + 1, :], gained)
    leaf_ref[...] = child.astype(jnp.int32)
    new_ref[...] = pred_ref[...] + 0.5 * gained


def solution(mesh):
    n_rows, n_feat = mesh.shape["rows"], mesh.shape["feat"]
    in_specs = (P("feat", "rows"), P("rows"), P("rows"), P("rows"), P("rows"), P(), P(), P("rows"))
    out_specs = (P("feat", "rows", None, None, None), P("rows"), P("rows"))
    vmem = pl.BlockSpec(memory_space=pltpu.VMEM)
    smem = pl.BlockSpec(memory_space=pltpu.SMEM)

    def body(bins, gradients, hessians, predictions, leaf, split_feature, split_bin, row_counts):
        width, rows_here = bins.shape
        leaves = split_feature.shape[0]
        kids = 2 * leaves
        owned = width // n_rows
        padded = round_up(owned, 8)
        chunks = rows_here // LANES
        small = round_up(chunks + 2, 16)
        cells = chunks * padded
        length = cells + 2 * small
        tall = (chunks, LANES)
        bf16 = jnp.bfloat16
        early, late = pl.pallas_call(
            functools.partial(exchange_kernel, (n_rows, n_feat, owned, padded, chunks, leaves)),
            out_shape=(jax.ShapeDtypeStruct((n_rows, length, LANES), bf16),
                       jax.ShapeDtypeStruct((n_rows, small, LANES), bf16)),
            in_specs=[pl.BlockSpec(memory_space=pl.ANY), vmem, vmem, vmem, smem, smem, smem],
            out_specs=(vmem, vmem),
            scratch_shapes=[
                pltpu.VMEM((width, rows_here), jnp.int32),
                pltpu.VMEM((n_rows, length, LANES), bf16),
                pltpu.VMEM((small, LANES), bf16),
                pltpu.VMEM((n_feat, small, LANES), bf16),
                pltpu.SemaphoreType.DMA,
                pltpu.SemaphoreType.DMA((n_feat - 1,)),
                pltpu.SemaphoreType.DMA((n_feat - 1,)),
                pltpu.SemaphoreType.DMA((n_rows - 1,)),
                pltpu.SemaphoreType.DMA((n_rows - 1,)),
                pltpu.SemaphoreType.DMA((n_rows - 1,)),
                pltpu.SemaphoreType.DMA((n_rows - 1,)),
            ],
            compiler_params=pltpu.CompilerParams(collective_id=0, has_side_effects=True,
                                                 vmem_limit_bytes=VMEM_BYTES),
            name="exchange_rows",
        )(bins, gradients.reshape(tall), hessians.reshape(tall), leaf.reshape(tall),
          split_feature, split_bin, row_counts)
        hist, new_leaf, new_pred = pl.pallas_call(
            functools.partial(histogram_kernel, (n_rows, owned, padded, chunks, kids)),
            out_shape=(jax.ShapeDtypeStruct((owned, 2 * kids, B), jnp.float32),
                       jax.ShapeDtypeStruct(tall, jnp.int32),
                       jax.ShapeDtypeStruct(tall, jnp.float32)),
            in_specs=[vmem, vmem, vmem],
            out_specs=(vmem, vmem, vmem),
            scratch_shapes=[pltpu.VMEM((n_rows + 1, 3 * small, LANES), jnp.float32),
                            pltpu.VMEM((2 * kids, LANES), jnp.float32),
                            pltpu.SMEM((n_rows * chunks // PAIR + GROUP,), jnp.int32)],
            compiler_params=pltpu.CompilerParams(vmem_limit_bytes=VMEM_BYTES),
            name="child_histograms",
        )(early, late, predictions.reshape(tall))
        return (hist.reshape(1, owned, 2, kids, B), new_leaf.reshape(rows_here), new_pred.reshape(rows_here))

    return jax.shard_map(body, mesh=mesh, in_specs=in_specs, out_specs=out_specs, check_vma=False)
```

```python
import functools

import jax
import jax.numpy as jnp
from jax import lax
from jax.experimental import pallas as pl
from jax.experimental.pallas import tpu as pltpu
from jax.sharding import PartitionSpec as P

B = 256
LANES = 128
HALF = 128
TILE = 16
PAIR = 2
GROUP = 4
MESH = pl.DeviceIdType.MESH


def round_up(value, unit):
    return -(-value // unit) * unit


def pad_rows(x, rows):
    if x.shape[0] == rows:
        return x
    return jnp.concatenate([x, jnp.zeros((rows - x.shape[0], x.shape[1]), x.dtype)], 0)


def exchange_kernel(dims, bins_hbm, grad_ref, hess_ref, leaf_ref, feature_ref, bin_ref, count_ref,
                    early_ref, late_ref, bins_ref, out_early, out_late, flag_in,
                    bins_sem, own_sem, flag_send, flag_recv, early_send, early_recv, late_send, late_recv):
    n_rows, n_feat, owned, padded, chunks, leaves = dims
    width = owned * n_rows
    me_r = lax.axis_index("rows")
    me_f = lax.axis_index("feat")
    small = out_late.shape[0]
    cells = chunks * padded

    def row_peer(step):
        return lax.rem(me_r + step, n_rows)

    def feat_peer(step):
        return lax.rem(me_f + step, n_feat)

    fetch = pltpu.make_async_copy(bins_hbm, bins_ref, bins_sem)
    fetch.start()
    barrier = pltpu.get_barrier_semaphore()
    for step in range(1, n_feat):
        pl.semaphore_signal(barrier, inc=1, device_id=(me_r, feat_peer(step)), device_id_type=MESH)
    for step in range(1, n_rows):
        pl.semaphore_signal(barrier, inc=1, device_id=(row_peer(step), me_f), device_id_type=MESH)

    leaf = leaf_ref[...]
    wanted = jnp.zeros(leaf.shape, jnp.int32)
    cutoff = jnp.zeros(leaf.shape, jnp.int32)
    for slot in range(leaves):
        here = leaf == slot
        wanted = jnp.where(here, feature_ref[slot], wanted)
        cutoff = jnp.where(here, bin_ref[slot], cutoff)
    local = wanted - me_f * width
    fetch.wait()
    ids = lax.broadcasted_iota(jnp.int32, (width, LANES), 0)
    chosen = []
    for chunk in range(chunks):
        block = bins_ref[:, chunk * LANES:(chunk + 1) * LANES]
        hit = ids == local[chunk:chunk + 1, :]
        chosen.append(jnp.sum(jnp.where(hit, block.astype(jnp.float32), 0.0), 0, keepdims=True))
    chosen = jnp.concatenate(chosen, 0)
    mine = (local >= 0) & (local < width)
    flags = jnp.where(mine & (chosen > cutoff.astype(jnp.float32)), 1.0, 0.0)
    flag_in[me_f] = pad_rows(flags, small).astype(jnp.bfloat16)

    count = count_ref[0]
    spot = (lax.broadcasted_iota(jnp.int32, leaf.shape, 0) * LANES
            + lax.broadcasted_iota(jnp.int32, leaf.shape, 1))
    live = spot < count
    upper = jnp.full((1, LANES), count // 8, jnp.int32).astype(jnp.float32)
    lower = jnp.full((1, LANES), count % 8, jnp.int32).astype(jnp.float32)
    grad = jnp.where(live, grad_ref[...].astype(jnp.float32), 0.0)
    hess = jnp.where(live, hess_ref[...].astype(jnp.float32), 0.0)
    tail = jnp.concatenate([pad_rows(jnp.concatenate([grad, upper, lower], 0), small),
                            pad_rows(hess, small)], 0).astype(jnp.bfloat16)
    for target in range(n_rows):
        blocks = []
        for chunk in range(chunks):
            block = bins_ref[target * owned:(target + 1) * owned, chunk * LANES:(chunk + 1) * LANES]
            blocks.append(pad_rows(block.astype(jnp.float32), padded))
        packed = jnp.concatenate(blocks, 0)
        out_early[target, :cells, :] = pad_rows(packed, cells).astype(jnp.bfloat16)
        out_early[target, cells:, :] = tail
    pl.semaphore_wait(barrier, n_feat - 1 + n_rows - 1)
    flag_copies = []
    for step in range(1, n_feat):
        copy = pltpu.make_async_remote_copy(
            src_ref=flag_in.at[me_f], dst_ref=flag_in.at[me_f],
            send_sem=flag_send.at[step - 1], recv_sem=flag_recv.at[step - 1],
            device_id=(me_r, feat_peer(step)), device_id_type=MESH)
        copy.start()
        flag_copies.append(copy)
    early_copies = []
    for step in range(1, n_rows):
        copy = pltpu.make_async_remote_copy(
            src_ref=out_early.at[row_peer(step)], dst_ref=early_ref.at[me_r],
            send_sem=early_send.at[step - 1], recv_sem=early_recv.at[step - 1],
            device_id=(row_peer(step), me_f), device_id_type=MESH)
        copy.start()
        early_copies.append(copy)

    for copy in flag_copies:
        copy.wait()
    merged = jnp.zeros((small, LANES), jnp.float32)
    for slot in range(n_feat):
        merged = merged + flag_in[slot].astype(jnp.float32)
    going = jnp.where(merged > 0.5, 1.0, 0.0)
    child = 2.0 * pad_rows(leaf.astype(jnp.float32), small) + going
    out_late[...] = child.astype(jnp.bfloat16)
    late_copies = []
    for step in range(1, n_rows):
        copy = pltpu.make_async_remote_copy(
            src_ref=out_late, dst_ref=late_ref.at[me_r],
            send_sem=late_send.at[step - 1], recv_sem=late_recv.at[step - 1],
            device_id=(row_peer(step), me_f), device_id_type=MESH)
        copy.start()
        late_copies.append(copy)
    own_copies = [pltpu.make_async_copy(out_early.at[me_r], early_ref.at[me_r], own_sem.at[0]),
                  pltpu.make_async_copy(out_late, late_ref.at[me_r], own_sem.at[1])]
    for copy in own_copies:
        copy.start()
    for copy in own_copies + early_copies + late_copies:
        copy.wait()


def histogram_kernel(dims, early_ref, late_ref, pred_ref, hist_ref, leaf_ref, new_ref, held, tot, order):
    n_rows, owned, padded, chunks, kids = dims
    cells = chunks * padded
    small = late_ref.shape[1]
    bf16 = jnp.bfloat16
    units = chunks // PAIR
    hist_ref[...] = jnp.zeros_like(hist_ref)
    tot[...] = jnp.zeros_like(tot)
    held[n_rows] = jnp.zeros(held.shape[1:], jnp.float32)
    for batch in range(n_rows):
        held[batch, :2 * small, :] = early_ref[batch, cells:, :].astype(jnp.float32)
        held[batch, 2 * small:, :] = late_ref[batch].astype(jnp.float32)
    filled = jnp.int32(0)
    for batch in range(n_rows):
        count = held[batch, chunks:chunks + 1, :] * 8.0 + held[batch, chunks + 1:chunks + 2, :]
        count = jnp.max(count).astype(jnp.int32)
        for unit in range(units):
            order[filled] = batch * units + unit
            filled = filled + jnp.where(count > unit * PAIR * LANES, 1, 0).astype(jnp.int32)
    for extra in range(GROUP):
        order[filled + extra] = n_rows * units

    rows16 = lax.broadcasted_iota(jnp.int32, (TILE, LANES), 0).astype(jnp.float32)
    levels = [(rows16 + float(TILE * at)).astype(bf16) for at in range(HALF // TILE)]
    slots = lax.broadcasted_iota(jnp.int32, (kids, LANES), 0).astype(jnp.float32).astype(bf16)
    one = jnp.ones((), bf16)
    zero = jnp.zeros((), bf16)

    def one_step(step, carry):
        highs, lows, weights = [], [], []
        for part in range(GROUP):
            number = order[step * GROUP + part]
            batch = number // units
            unit = number - batch * units
            source = jnp.minimum(batch, n_rows - 1)
            start = pl.multiple_of(unit * PAIR * padded, PAIR * padded)
            block = early_ref[source, pl.ds(start, PAIR * padded), :].astype(jnp.float32)
            high = jnp.where(block >= float(HALF), 1.0, 0.0)
            low = block - high * float(HALF)
            for half in range(PAIR):
                highs.append(high[half * padded:(half + 1) * padded])
                lows.append(low[half * padded:(half + 1) * padded])
                chunk = unit * PAIR + half
                grad, hess, child = [
                    jnp.broadcast_to(held[batch, pl.ds(chunk + small * kind, 1), :], (kids, LANES)).astype(bf16)
                    for kind in range(3)]
                member = slots == child
                weights.append(jnp.concatenate([jnp.where(member, grad, zero), jnp.where(member, hess, zero)], 0))
        tot[...] += sum(w.astype(jnp.float32) for w in weights)
        both = jnp.concatenate(weights, 1)
        for f in range(owned):
            hot = []
            top = []
            for high, low in zip(highs, lows):
                level = jnp.broadcast_to(low[f:f + 1, :], (TILE, LANES)).astype(bf16)
                hot.append(jnp.concatenate([jnp.where(level == at, one, zero) for at in levels], 0))
                top.append(jnp.broadcast_to(high[f:f + 1, :], (2 * kids, LANES)).astype(bf16))
            hot = jnp.concatenate(hot, 1)
            upper = both * jnp.concatenate(top, 1)
            masked = jnp.concatenate([both - upper, upper], 0)
            found = lax.dot_general(masked, hot, (((1,), (1,)), ((), ())),
                                    preferred_element_type=jnp.float32)
            hist_ref[f, :, :HALF] += found[:2 * kids]
            hist_ref[f, :, HALF:] += found[2 * kids:]
        return carry

    lax.fori_loop(0, (filled + GROUP - 1) // GROUP, one_step, 0)

    totals = jnp.sum(tot[...], 1, keepdims=True)
    value = -totals[:kids] / (totals[kids:] + 1.0)
    me_r = lax.axis_index("rows")
    child = held[me_r, 2 * small:2 * small + chunks, :]
    gained = jnp.zeros(child.shape, jnp.float32)
    for kid in range(kids):
        gained = jnp.where(child == float(kid), value[kid:kid + 1, :], gained)
    leaf_ref[...] = child.astype(jnp.int32)
    new_ref[...] = pred_ref[...] + 0.5 * gained


def solution(mesh):
    n_rows, n_feat = mesh.shape["rows"], mesh.shape["feat"]
    in_specs = (P("feat", "rows"), P("rows"), P("rows"), P("rows"), P("rows"), P(), P(), P("rows"))
    out_specs = (P("feat", "rows", None, None, None), P("rows"), P("rows"))
    vmem = pl.BlockSpec(memory_space=pltpu.VMEM)
    smem = pl.BlockSpec(memory_space=pltpu.SMEM)
    hbm = pl.BlockSpec(memory_space=pl.ANY)

    def body(bins, gradients, hessians, predictions, leaf, split_feature, split_bin, row_counts):
        width, rows_here = bins.shape
        leaves = split_feature.shape[0]
        kids = 2 * leaves
        owned = width // n_rows
        padded = round_up(owned, 8)
        chunks = rows_here // LANES
        small = round_up(chunks + 2, 16)
        cells = chunks * padded
        length = cells + 2 * small
        tall = (chunks, LANES)
        bf16 = jnp.bfloat16
        early, late = pl.pallas_call(
            functools.partial(exchange_kernel, (n_rows, n_feat, owned, padded, chunks, leaves)),
            out_shape=(jax.ShapeDtypeStruct((n_rows, length, LANES), bf16),
                       jax.ShapeDtypeStruct((n_rows, small, LANES), bf16)),
            in_specs=[hbm, vmem, vmem, vmem, smem, smem, smem],
            out_specs=(hbm, hbm),
            scratch_shapes=[
                pltpu.VMEM((width, rows_here), jnp.int32),
                pltpu.VMEM((n_rows, length, LANES), bf16),
                pltpu.VMEM((small, LANES), bf16),
                pltpu.VMEM((n_feat, small, LANES), bf16),
                pltpu.SemaphoreType.DMA,
                pltpu.SemaphoreType.DMA((2,)),
                pltpu.SemaphoreType.DMA((n_feat - 1,)),
                pltpu.SemaphoreType.DMA((n_feat - 1,)),
                pltpu.SemaphoreType.DMA((n_rows - 1,)),
                pltpu.SemaphoreType.DMA((n_rows - 1,)),
                pltpu.SemaphoreType.DMA((n_rows - 1,)),
                pltpu.SemaphoreType.DMA((n_rows - 1,)),
            ],
            compiler_params=pltpu.CompilerParams(collective_id=0, has_side_effects=True),
            name="exchange_rows",
        )(bins, gradients.reshape(tall), hessians.reshape(tall), leaf.reshape(tall),
          split_feature, split_bin, row_counts)
        hist, new_leaf, new_pred = pl.pallas_call(
            functools.partial(histogram_kernel, (n_rows, owned, padded, chunks, kids)),
            out_shape=(jax.ShapeDtypeStruct((owned, 2 * kids, B), jnp.float32),
                       jax.ShapeDtypeStruct(tall, jnp.int32),
                       jax.ShapeDtypeStruct(tall, jnp.float32)),
            in_specs=[vmem, vmem, vmem],
            out_specs=(vmem, vmem, vmem),
            scratch_shapes=[pltpu.VMEM((n_rows + 1, 3 * small, LANES), jnp.float32),
                            pltpu.VMEM((2 * kids, LANES), jnp.float32),
                            pltpu.SMEM((n_rows * chunks // PAIR + GROUP,), jnp.int32)],
            name="child_histograms",
        )(early, late, predictions.reshape(tall))
        return (hist.reshape(1, owned, 2, kids, B), new_leaf.reshape(rows_here), new_pred.reshape(rows_here))

    return jax.shard_map(body, mesh=mesh, in_specs=in_specs, out_specs=out_specs, check_vma=False)
```
